512 devices in a mesh: cfg: 8 (over z_hi, x), col: 64 (over y, z_lo, core).
Axes of the slice: x: 4, y: 4, z: 16 (z_hi: 2, z_lo: 8; z = z_hi * 8 + z_lo), core: 2. Of those that a mesh axis runs over, the one named last changes fastest.
Arguments:
- band_values: bfloat16 [3, 16384, 1024], P(None, ('cfg', 'col')), may hold values from -0.1875 to 0.1875
- initial_vectors: bfloat16 [16384, 1024], P(('cfg', 'col')), may hold values from -0.1875 to 0.1875
- final_vectors: bfloat16 [6144, 16384], P('col', 'cfg'), may hold values from -6 to 6
- band_offsets: int32 [256], P('cfg'), may hold values from 0 to 15360, as said below
Outputs:
- dipole: bfloat16 [3, 6144, 1024], P(None, 'col', 'cfg')
The draws below stay inside these ranges and needn't reach their ends.
Inputs may be any that keep to these rules, and one draw needn't show every extreme that they name: `band_offsets`: the band of configuration block b begins within 32 of b * 64 + 64 // 2 - 1024 // 2, clipped to the matrix.
All inputs are finite; a program needn't handle non-finite values.
Results may differ from the reference program's by a relative error of at most 0.0049.
Values may be sent and summed in bfloat16 or wider, within the bound.
No kernel may reach another device: no remote copies, remote signals or barrier semaphores. Data moves between devices by JAX's collectives and lax.ppermute only.
A program may use at most 64 MiB of HBM per device.

```python
import jax
import jax.numpy as jnp
from jax import lax

COMP = 3
W = 1024
BLK = 64
NI = 1024
NF = 6144
N = 16384


def draw_band_offsets(key, part):
    block_count = N // BLK
    centers = jnp.arange(block_count, dtype=jnp.int32) * BLK + BLK // 2 - W // 2
    jitter = jax.random.randint(key, (block_count,), -(BLK // 2), BLK // 2 + 1, dtype=jnp.int32)
    return jnp.clip(centers + jitter, 0, N - W).astype(jnp.int32)


def raised(array, key, source, target, parts, factor):
    owner, partner = [(jnp.arange(array.shape[dim]) // (array.shape[dim] // parts)).reshape([-1 if axis == dim else 1 for axis in range(array.ndim)]) for dim in (source, target)]
    chosen = jax.random.permutation(key, parts)[partner]
    strong = (owner == chosen) | (owner == (partner + parts // 2) % parts)
    return jnp.where(strong, factor * array, array)


def level_of(rng, dims, pieces, smallest, largest):
    level, own = 1.0, jax.random.fold_in(rng, 6)
    for axis_at, parts in pieces:
        steps = jnp.exp(jax.random.uniform(jax.random.fold_in(own, axis_at), (parts,), jnp.float32, smallest / len(pieces), largest / len(pieces)))
        level = level * jnp.repeat(steps, dims[axis_at] // parts).reshape([-1 if axis == axis_at else 1 for axis in range(len(dims))])
    return level


def scatter_about(own_key, shape, deviation, reach, pieces=(), held_as=jnp.bfloat16):
    factor_of = level_of(own_key, shape, pieces, -0.22, 0.18) if pieces else 1.0
    array = jax.random.normal(own_key, shape, jnp.float32) * deviation * factor_of
    return jnp.minimum(jnp.maximum(array, -reach), reach).astype(held_as)


def noise_with(stream_key, dims, deviation, bound, cuts, heavy, kind=jnp.bfloat16):
    result = deviation * jax.random.normal(stream_key, dims, jnp.float32)
    if cuts:
        result = result * level_of(stream_key, dims, cuts, -0.22, 0.18)
    return jnp.clip(raised(result, jax.random.fold_in(stream_key, 3), *heavy), -bound, bound).astype(kind)


def setup_inputs(seed: int = 0) -> dict:
    key_list = jax.random.split(jax.random.key(seed), 5)
    band_values = scatter_about(key_list[0], (COMP, N, W), W ** -0.5, 0.1875, ((1, 512),))
    initial_vectors = noise_with(key_list[1], (N, NI), N ** -0.5, 0.1875, ((0, 512),), (0, 1, 512, 6.0))
    final_vectors = scatter_about(key_list[2], (NF, N), 1.0, 6.0, ((0, 64), (1, 8)))
    band_offsets = draw_band_offsets(jax.random.fold_in(key_list[4], 71), 0)
    return {"band_values": band_values, "initial_vectors": initial_vectors, "final_vectors": final_vectors, "band_offsets": band_offsets}


def reference(band_values, initial_vectors, final_vectors, band_offsets):
    block_count = band_offsets.shape[0]
    blocks = jnp.transpose(band_values.reshape(COMP, block_count, BLK, W), (1, 0, 2, 3))

    def project_block(packed):
        block_vals, first_col = packed
        window = lax.dynamic_slice_in_dim(final_vectors, first_col.astype(jnp.int32), W, 1)
        return jnp.einsum('pkw,cw->pck', block_vals.astype(jnp.float32), window.astype(jnp.float32)).astype(jnp.bfloat16)

    applied = lax.map(project_block, (blocks, band_offsets))
    applied = jnp.transpose(applied, (1, 2, 0, 3)).reshape(COMP, NF, block_count * BLK)
    results = [jnp.dot(applied[comp], initial_vectors, preferred_element_type=jnp.float32) for comp in range(COMP)]
    return jnp.stack(results).astype(jnp.bfloat16)
```

```python
import functools

import jax
import jax.numpy as jnp
from jax import lax
from jax.experimental import pallas as pl
from jax.experimental.pallas import tpu as pltpu
from jax.sharding import Mesh
from jax.sharding import PartitionSpec as P

BLK = 64
HALF = 512
AXES = ("zh", "x", "y", "zl", "core")
ORDER = (0, 4, 2, 6, 1, 5, 3, 7)


def roll_kernel(start_ref, band_ref, vec_ref, out_ref):
    comps = band_ref.shape[0]
    for p in range(comps):
        rows = band_ref[p].astype(jnp.float32)
        out_ref[p] = pltpu.roll(rows, start_ref[0], 1).astype(out_ref.dtype)
    out_ref[comps] = vec_ref[...]


def product_kernel(starts_ref, panel_ref, *refs):
    pieces, out_ref, band_s, vec_s = refs[:-3], refs[-3], refs[-2], refs[-1]
    p = pl.program_id(0)
    rows, width = pieces[0].shape[1:]
    lane = lax.broadcasted_iota(jnp.int32, (rows, HALF), 1)
    for n, ref in enumerate(pieces):
        at = pl.ds(n * rows, rows)
        start = starts_ref[n // 2]
        low = ref[p, :, :HALF]
        zero = jnp.zeros_like(low)
        band_s[at, :HALF] = jnp.where(lane >= start, low, zero)
        band_s[at, HALF:width] = ref[p, :, HALF:]
        band_s[at, width:] = jnp.where(lane < start, low, zero)
        vec_s[at, :] = ref[3]
    quarters, lines = panel_ref.shape[:2]
    panel = panel_ref[...].reshape(quarters * lines, panel_ref.shape[2])
    applied = lax.dot_general(
        panel, band_s[...], (((1,), (1,)), ((), ())), preferred_element_type=jnp.float32
    ).astype(jnp.bfloat16)
    sums = jnp.dot(applied, vec_s[...], preferred_element_type=jnp.float32)
    out_ref[...] = sums.reshape(out_ref.shape).astype(out_ref.dtype)


def shards(band_values, initial_vectors, final_vectors, band_offsets):
    comps, own_rows, width = band_values.shape
    lines, row_count = final_vectors.shape
    vectors = initial_vectors.shape[1]
    zh, x, y, zl = (lax.axis_index(a) for a in AXES[:4])
    panel_start = (zh * 4 + x) * row_count + (y - 1) * HALF
    order = jnp.array(ORDER, jnp.int32) ^ zl
    starts = jnp.take(band_offsets, y * 8 + order, mode="clip") - panel_start

    up = [(i, i + 1) for i in range(7)]
    down = [(i + 1, i) for i in range(7)]
    before = lax.ppermute(final_vectors[:, row_count - HALF :], ("zh", "x"), up)
    after = lax.ppermute(final_vectors[:, :HALF], ("zh", "x"), down)

    own = pl.pallas_call(
        roll_kernel,
        out_shape=jax.ShapeDtypeStruct((comps + 1, own_rows, width), jnp.bfloat16),
        in_specs=[
            pl.BlockSpec(memory_space=pltpu.SMEM),
            pl.BlockSpec(memory_space=pltpu.VMEM),
            pl.BlockSpec(memory_space=pltpu.VMEM),
        ],
        out_specs=pl.BlockSpec(memory_space=pltpu.VMEM),
        name="roll",
    )(starts, band_values, initial_vectors)

    def along_z(block, step):
        return lax.ppermute(block, "zl", [(i, i ^ step) for i in range(8)])

    def other_core(block):
        return lax.ppermute(block, "core", [(0, 1), (1, 0)])

    blocks = [own]
    for step in (4, 2, 1):
        blocks = blocks + [along_z(b, step) for b in blocks]
    pieces = []
    for b in blocks:
        pieces += [b, other_core(b)]

    wide = jnp.concatenate([before, final_vectors, after], axis=1)
    windows = jnp.stack([wide[:, HALF * k : HALF * (k + 3)] for k in range(4)])
    panel = lax.all_to_all(windows, "y", 0, 0)

    vmem = pl.BlockSpec(memory_space=pltpu.VMEM)
    depth = len(pieces) * own_rows
    sums = pl.pallas_call(
        product_kernel,
        grid=(comps,),
        out_shape=jax.ShapeDtypeStruct((4, comps, lines, vectors), jnp.bfloat16),
        in_specs=[pl.BlockSpec(memory_space=pltpu.SMEM), vmem] + [vmem] * len(pieces),
        out_specs=pl.BlockSpec((4, 1, lines, vectors), lambda p: (0, p, 0, 0)),
        scratch_shapes=[
            pltpu.VMEM((depth, 3 * HALF), jnp.bfloat16),
            pltpu.VMEM((depth, vectors), jnp.bfloat16),
        ],
        compiler_params=pltpu.CompilerParams(vmem_limit_bytes=32 * 1024 * 1024),
        cost_estimate=pl.CostEstimate(
            flops=2 * comps * 4 * lines * depth * (3 * HALF + vectors), bytes_accessed=12_000_000, transcendentals=0
        ),
        name="product",
    )(starts, panel, *pieces)

    def add_up(parts):
        return jnp.sum(parts.astype(jnp.float32), axis=0)

    over_y = add_up(lax.all_to_all(sums, "y", 0, 0)).astype(jnp.bfloat16)
    over_y = over_y.reshape(comps, lines, 2, 4, vectors // 8).transpose(3, 2, 0, 1, 4)
    over_x = add_up(lax.all_to_all(over_y, "x", 0, 0))
    mine = jnp.where(zh == 0, over_x[0], over_x[1])
    theirs = jnp.where(zh == 0, over_x[1], over_x[0]).astype(jnp.bfloat16)
    got = lax.ppermute(theirs, "zh", [(0, 1), (1, 0)])
    return (mine + got.astype(jnp.float32)).astype(jnp.bfloat16)


def solution(mesh):
    fine = Mesh(mesh.devices.reshape(2, 4, 4, 8, 2), AXES)
    cfg, col = AXES[:2], AXES[2:]
    placed = (P(None, AXES, None), P(AXES, None), P(col, cfg), P(cfg))
    return jax.shard_map(
        shards, mesh=fine, in_specs=placed, out_specs=P(None, col, cfg), check_vma=False
    )
```

```python
import functools

import jax
import jax.numpy as jnp
from jax import lax
from jax.experimental import pallas as pl
from jax.experimental.pallas import tpu as pltpu
from jax.sharding import Mesh
from jax.sharding import PartitionSpec as P

BLK = 64
HALF = 512
AXES = ("zh", "x", "y", "zl", "core")
ORDER = (0, 4, 2, 6, 1, 5, 3, 7)
VMEM = pl.BlockSpec(memory_space=pltpu.VMEM)
SMEM = pl.BlockSpec(memory_space=pltpu.SMEM)


def panel_start(row_count):
    zh, x, y = (lax.axis_index(a) for a in AXES[:3])
    return (zh * 4 + x) * row_count + (y - 1) * HALF


def roll_kernel(offsets_ref, band_ref, vec_ref, fin_ref, head_ref, tail_ref, last_ref, first_ref):
    row_count = fin_ref.shape[1]
    start = offsets_ref[lax.axis_index("y") * 8 + lax.axis_index("zl")] - panel_start(row_count)

    def rolled(p):
        return pltpu.roll(band_ref[p].astype(jnp.float32), start, 1).astype(jnp.bfloat16)

    head_ref[0, 0] = vec_ref[...]
    head_ref[0, 1] = rolled(0)
    tail_ref[0, 0] = rolled(1)
    tail_ref[0, 1] = rolled(2)
    last_ref[...] = fin_ref[:, row_count - HALF :]
    first_ref[...] = fin_ref[:, :HALF]


def product_kernel(row_count, count, offsets_ref, panel_ref, *refs):
    vecs, bands, out_ref, band_s, vec_s = refs[:4], refs[4:-3], refs[-3], refs[-2], refs[-1]
    bands = bands or vecs
    p = pl.program_id(0) + (2 - count)
    blocks, _, rows, width = vecs[0].shape
    base, zl = lax.axis_index("y") * 8, lax.axis_index("zl")
    lane = lax.broadcasted_iota(jnp.int32, (rows, HALF), 1)
    for a in range(4):
        for n in range(blocks):
            at = pl.ds((a * blocks + n) * rows, rows)
            start = offsets_ref[base + (zl ^ ORDER[a // 2 * blocks + n])] - panel_start(row_count)
            low = bands[a][n, p, :, :HALF]
            zero = jnp.zeros_like(low)
            band_s[at, :HALF] = jnp.where(lane >= start, low, zero)
            band_s[at, HALF:width] = bands[a][n, p, :, HALF:]
            band_s[at, width:] = jnp.where(lane < start, low, zero)
            vec_s[at, :] = vecs[a][n, 0]
    quarters, lines = panel_ref.shape[:2]
    panel = panel_ref[...].reshape(quarters * lines, panel_ref.shape[2])
    applied = lax.dot_general(
        panel, band_s[...], (((1,), (1,)), ((), ())), preferred_element_type=jnp.float32
    ).astype(jnp.bfloat16)
    sums = jnp.dot(applied, vec_s[...], preferred_element_type=jnp.float32).astype(out_ref.dtype)
    lanes = out_ref.shape[-1]
    for dx in range(4):
        for dy in range(4):
            for dz in range(2):
                out_ref[dx * 4 + dy, 0, dz] = sums[
                    dy * lines : (dy + 1) * lines, (dz * 4 + dx) * lanes : (dz * 4 + dx + 1) * lanes
                ]


def shards(band_values, initial_vectors, final_vectors, band_offsets):
    comps, own_rows, width = band_values.shape
    lines, row_count = final_vectors.shape
    vectors = initial_vectors.shape[1]
    zh = lax.axis_index("zh")
    bf16 = jnp.bfloat16

    half = jax.ShapeDtypeStruct((1, 2, own_rows, width), bf16)
    edge = jax.ShapeDtypeStruct((lines, HALF), bf16)
    head, tail, last, first = pl.pallas_call(
        roll_kernel,
        out_shape=(half, half, edge, edge),
        in_specs=[SMEM, VMEM, VMEM, VMEM],
        out_specs=(VMEM, VMEM, VMEM, VMEM),
        name="roll",
    )(band_offsets, band_values, initial_vectors, final_vectors)

    def along_z(blocks, step):
        return lax.ppermute(blocks, "zl", [(i, i ^ step) for i in range(8)])

    def other_core(blocks):
        return lax.ppermute(blocks, "core", [(0, 1), (1, 0)])

    def gathered(own):
        two = jnp.concatenate([own, along_z(own, 4)])
        near = jnp.concatenate([two, along_z(two, 2)])
        far = along_z(near, 1)
        return [near, other_core(near), far, other_core(far)]

    head_blocks = gathered(head)
    tail_blocks = gathered(tail)

    before = lax.ppermute(last, ("zh", "x"), [(i, i + 1) for i in range(7)])
    after = lax.ppermute(first, ("zh", "x"), [(i + 1, i) for i in range(7)])
    wide = jnp.concatenate([before, final_vectors, after], axis=1)
    windows = jnp.stack([wide[:, HALF * k : HALF * (k + 3)] for k in range(4)])
    panel = lax.all_to_all(windows, "y", 0, 0)

    def product(count, vecs, bands):
        depth = 16 * own_rows
        return pl.pallas_call(
            functools.partial(product_kernel, row_count, count),
            grid=(count,),
            out_shape=jax.ShapeDtypeStruct((16, count, 2, lines, vectors // 8), bf16),
            in_specs=[SMEM, VMEM] + [VMEM] * (len(vecs) + len(bands)),
            out_specs=pl.BlockSpec((16, 1, 2, lines, vectors // 8), lambda p: (0, p, 0, 0, 0)),
            scratch_shapes=[pltpu.VMEM((depth, 3 * HALF), bf16), pltpu.VMEM((depth, vectors), bf16)],
            compiler_params=pltpu.CompilerParams(vmem_limit_bytes=24 * 1024 * 1024),
            cost_estimate=pl.CostEstimate(
                flops=2 * count * 4 * lines * depth * (3 * HALF + vectors),
                bytes_accessed=4_000_000 * count,
                transcendentals=0,
            ),
            name=f"product_{count}",
        )(band_offsets, panel, *vecs, *bands)

    def summed(partial):
        parts = lax.all_to_all(partial, ("x", "y"), 0, 0)
        total = jnp.sum(parts.astype(jnp.float32), axis=0)
        mine = jnp.where(zh == 0, total[:, 0], total[:, 1])
        theirs = jnp.where(zh == 0, total[:, 1], total[:, 0]).astype(bf16)
        got = lax.ppermute(theirs, "zh", [(0, 1), (1, 0)])
        return (mine + got.astype(jnp.float32)).astype(bf16)

    first_sum = summed(product(1, head_blocks, []))
    rest_sum = summed(product(2, head_blocks, tail_blocks))
    return jnp.concatenate([first_sum, rest_sum])


def solution(mesh):
    fine = Mesh(mesh.devices.reshape(2, 4, 4, 8, 2), AXES)
    cfg, col = AXES[:2], AXES[2:]
    placed = (P(None, AXES, None), P(AXES, None), P(col, cfg), P(cfg))
    return jax.shard_map(
        shards, mesh=fine, in_specs=placed, out_specs=P(None, col, cfg), check_vma=False
    )
```

```python
import functools

import jax
import jax.numpy as jnp
from jax import lax
from jax.experimental import pallas as pl
from jax.experimental.pallas import tpu as pltpu
from jax.sharding import Mesh
from jax.sharding import PartitionSpec as P

BLK = 64
HALF = 512
AXES = ("zh", "x", "y", "zl", "core")
ORDER = (0, 4, 2, 6, 1, 5, 3, 7)
VMEM = pl.BlockSpec(memory_space=pltpu.VMEM)
SMEM = pl.BlockSpec(memory_space=pltpu.SMEM)
SMALL = pltpu.CompilerParams(vmem_limit_bytes=4 * 1024 * 1024)


def panel_start(row_count):
    zh, x, y = (lax.axis_index(a) for a in AXES[:3])
    return (zh * 4 + x) * row_count + (y - 1) * HALF


def roll_kernel(offsets_ref, band_ref, vec_ref, fin_ref, own_ref, last_ref, first_ref):
    row_count = fin_ref.shape[1]
    start = offsets_ref[lax.axis_index("y") * 8 + lax.axis_index("zl")] - panel_start(row_count)

    def rolled(p):
        return pltpu.roll(band_ref[p].astype(jnp.float32), start, 1).astype(jnp.bfloat16)

    own_ref[0, 0] = vec_ref[...]
    for p in range(band_ref.shape[0]):
        own_ref[0, p + 1] = rolled(p)
    last_ref[...] = fin_ref[:, row_count - HALF :]
    first_ref[...] = fin_ref[:, :HALF]


def pair_kernel(own_ref, got_ref, before_ref, fin_ref, after_ref, two_ref, windows_ref):
    two_ref[:1] = own_ref[...]
    two_ref[1:] = got_ref[...]
    quarters = windows_ref.shape[0]
    for k in range(quarters):
        for c in range(3):
            source, at = fin_ref, k + c - 1
            if at < 0:
                source, at = before_ref, 0
            elif at == quarters:
                source, at = after_ref, 0
            windows_ref[k, :, c * HALF : (c + 1) * HALF] = source[:, at * HALF : (at + 1) * HALF]


def near_kernel(two_ref, more_ref, panel_ref, out_ref):
    out_ref[:2] = two_ref[...]
    out_ref[2:] = more_ref[...]


def product_kernel(row_count, first, offsets_ref, panel_ref, *refs):
    pieces, out_ref, band_s, vec_s = refs[:-3], refs[-3], refs[-2], refs[-1]
    p = pl.program_id(0) + first + 1
    blocks, _, rows, width = pieces[0].shape
    base, zl = lax.axis_index("y") * 8, lax.axis_index("zl")
    lane = lax.broadcasted_iota(jnp.int32, (rows, HALF), 1)
    for a in range(4):
        for n in range(blocks):
            at = pl.ds((a * blocks + n) * rows, rows)
            start = offsets_ref[base + (zl ^ ORDER[a // 2 * blocks + n])] - panel_start(row_count)
            low = pieces[a][n, p, :, :HALF]
            zero = jnp.zeros_like(low)
            band_s[at, :HALF] = jnp.where(lane >= start, low, zero)
            band_s[at, HALF:width] = pieces[a][n, p, :, HALF:]
            band_s[at, width:] = jnp.where(lane < start, low, zero)
            vec_s[at, :] = pieces[a][n, 0]
    quarters, lines = panel_ref.shape[:2]
    panel = panel_ref[...].reshape(quarters * lines, panel_ref.shape[2])
    applied = lax.dot_general(
        panel, band_s[...], (((1,), (1,)), ((), ())), preferred_element_type=jnp.float32
    ).astype(jnp.bfloat16)
    sums = jnp.dot(applied, vec_s[...], preferred_element_type=jnp.float32).astype(out_ref.dtype)
    lanes = out_ref.shape[-1]
    for dx in range(4):
        for dy in range(4):
            for dz in range(2):
                out_ref[dx * 4 + dy, 0, dz] = sums[
                    dy * lines : (dy + 1) * lines, (dz * 4 + dx) * lanes : (dz * 4 + dx + 1) * lanes
                ]


def shards(band_values, initial_vectors, final_vectors, band_offsets):
    comps, own_rows, width = band_values.shape
    lines, row_count = final_vectors.shape
    vectors = initial_vectors.shape[1]
    zh = lax.axis_index("zh")
    bf16 = jnp.bfloat16

    block = jax.ShapeDtypeStruct((1, comps + 1, own_rows, width), bf16)
    edge = jax.ShapeDtypeStruct((lines, HALF), bf16)
    own, last, first = pl.pallas_call(
        roll_kernel,
        out_shape=(block, edge, edge),
        in_specs=[SMEM, VMEM, VMEM, VMEM],
        out_specs=(VMEM, VMEM, VMEM),
        compiler_params=SMALL,
        name="roll",
    )(band_offsets, band_values, initial_vectors, final_vectors)

    def along_z(blocks, step):
        return lax.ppermute(blocks, "zl", [(i, i ^ step) for i in range(8)])

    def other_core(blocks):
        return lax.ppermute(blocks, "core", [(0, 1), (1, 0)])

    before = lax.ppermute(last, ("zh", "x"), [(i, i + 1) for i in range(7)])
    after = lax.ppermute(first, ("zh", "x"), [(i + 1, i) for i in range(7)])
    two, windows = pl.pallas_call(
        pair_kernel,
        out_shape=(
            jax.ShapeDtypeStruct((2, comps + 1, own_rows, width), bf16),
            jax.ShapeDtypeStruct((4, lines, 3 * HALF), bf16),
        ),
        in_specs=[VMEM] * 5,
        out_specs=(VMEM, VMEM),
        compiler_params=SMALL,
        name="pair",
    )(own, along_z(own, 4), before, final_vectors, after)
    panel = lax.all_to_all(windows, "y", 0, 0)

    near = pl.pallas_call(
        near_kernel,
        out_shape=jax.ShapeDtypeStruct((4, comps + 1, own_rows, width), bf16),
        in_specs=[VMEM, VMEM, VMEM],
        out_specs=VMEM,
        compiler_params=SMALL,
        name="near",
    )(two, along_z(two, 2), panel)
    far = along_z(near, 1)
    blocks = [near, other_core(near), far, other_core(far)]

    def product(first, count):
        depth = 16 * own_rows
        return pl.pallas_call(
            functools.partial(product_kernel, row_count, first),
            grid=(count,),
            out_shape=jax.ShapeDtypeStruct((16, count, 2, lines, vectors // 8), bf16),
            in_specs=[SMEM, VMEM] + [VMEM] * len(blocks),
            out_specs=pl.BlockSpec((16, 1, 2, lines, vectors // 8), lambda p: (0, p, 0, 0, 0)),
            scratch_shapes=[pltpu.VMEM((depth, 3 * HALF), bf16), pltpu.VMEM((depth, vectors), bf16)],
            compiler_params=pltpu.CompilerParams(vmem_limit_bytes=16 * 1024 * 1024),
            cost_estimate=pl.CostEstimate(
                flops=2 * count * 4 * lines * depth * (3 * HALF + vectors),
                bytes_accessed=4_000_000 * count,
                transcendentals=0,
            ),
            name=f"product_{count}",
        )(band_offsets, panel, *blocks)

    def summed(partial):
        parts = lax.all_to_all(partial, ("x", "y"), 0, 0)
        total = jnp.sum(parts.astype(jnp.float32), axis=0)
        mine = jnp.where(zh == 0, total[:, 0], total[:, 1])
        theirs = jnp.where(zh == 0, total[:, 1], total[:, 0]).astype(bf16)
        got = lax.ppermute(theirs, "zh", [(0, 1), (1, 0)])
        return (mine + got.astype(jnp.float32)).astype(bf16)

    first_sum = summed(product(0, 1))
    rest_sum = summed(product(1, 2))
    return jnp.concatenate([first_sum, rest_sum])


def solution(mesh):
    fine = Mesh(mesh.devices.reshape(2, 4, 4, 8, 2), AXES)
    cfg, col = AXES[:2], AXES[2:]
    placed = (P(None, AXES, None), P(AXES, None), P(col, cfg), P(cfg))
    return jax.shard_map(
        shards, mesh=fine, in_specs=placed, out_specs=P(None, col, cfg), check_vma=False
    )
```

```python
import functools

import jax
import jax.numpy as jnp
from jax import lax
from jax.experimental import pallas as pl
from jax.experimental.pallas import tpu as pltpu
from jax.sharding import Mesh
from jax.sharding import PartitionSpec as P

BLK = 64
HALF = 512
AXES = ("zh", "x", "y", "zl", "core")
ORDER = (0, 4, 2, 6, 1, 5, 3, 7)
VMEM = pl.BlockSpec(memory_space=pltpu.VMEM)
SMEM = pl.BlockSpec(memory_space=pltpu.SMEM)


def panel_start(row_count):
    zh, x, y = (lax.axis_index(a) for a in AXES[:3])
    return (zh * 4 + x) * row_count + (y - 1) * HALF


def roll_kernel(offsets_ref, band_ref, vec_ref, head_ref, tail_ref, *, row_count):
    start = offsets_ref[lax.axis_index("y") * 8 + lax.axis_index("zl")] - panel_start(row_count)

    def rolled(p):
        return pltpu.roll(band_ref[p].astype(jnp.float32), start, 1).astype(jnp.bfloat16)

    head_ref[0, 0] = vec_ref[...]
    head_ref[0, 1] = rolled(0)
    tail_ref[0, 0] = rolled(1)
    tail_ref[0, 1] = rolled(2)


def product_kernel(row_count, count, offsets_ref, panel_ref, *refs):
    vecs, bands, out_ref, band_s, vec_s = refs[:4], refs[4:-3], refs[-3], refs[-2], refs[-1]
    bands = bands or vecs
    p = pl.program_id(0) + (2 - count)
    blocks, _, rows, width = vecs[0].shape
    base, zl = lax.axis_index("y") * 8, lax.axis_index("zl")
    lane = lax.broadcasted_iota(jnp.int32, (rows, HALF), 1)
    for a in range(4):
        for n in range(blocks):
            at = pl.ds((a * blocks + n) * rows, rows)
            start = offsets_ref[base + (zl ^ ORDER[a // 2 * blocks + n])] - panel_start(row_count)
            low = bands[a][n, p, :, :HALF]
            zero = jnp.zeros_like(low)
            band_s[at, :HALF] = jnp.where(lane >= start, low, zero)
            band_s[at, HALF:width] = bands[a][n, p, :, HALF:]
            band_s[at, width:] = jnp.where(lane < start, low, zero)
            vec_s[at, :] = vecs[a][n, 0]
    quarters, lines = panel_ref.shape[:2]
    panel = panel_ref[...].reshape(quarters * lines, panel_ref.shape[2])
    applied = lax.dot_general(
        panel, band_s[...], (((1,), (1,)), ((), ())), preferred_element_type=jnp.float32
    ).astype(jnp.bfloat16)
    sums = jnp.dot(applied, vec_s[...], preferred_element_type=jnp.float32).astype(out_ref.dtype)
    lanes = out_ref.shape[-1]
    for dx in range(4):
        for dy in range(4):
            for dz in range(2):
                out_ref[dx * 4 + dy, 0, dz] = sums[
                    dy * lines : (dy + 1) * lines, (dz * 4 + dx) * lanes : (dz * 4 + dx + 1) * lanes
                ]


def shards(band_values, initial_vectors, final_vectors, band_offsets):
    comps, own_rows, width = band_values.shape
    lines, row_count = final_vectors.shape
    vectors = initial_vectors.shape[1]
    zh = lax.axis_index("zh")
    bf16 = jnp.bfloat16

    half = jax.ShapeDtypeStruct((1, 2, own_rows, width), bf16)
    head, tail = pl.pallas_call(
        functools.partial(roll_kernel, row_count=row_count),
        out_shape=(half, half),
        in_specs=[SMEM, VMEM, VMEM],
        out_specs=(VMEM, VMEM),
        name="roll",
    )(band_offsets, band_values, initial_vectors)

    def along_z(blocks, step):
        return lax.ppermute(blocks, "zl", [(i, i ^ step) for i in range(8)])

    def other_core(blocks):
        return lax.ppermute(blocks, "core", [(0, 1), (1, 0)])

    def gathered(own):
        two = jnp.concatenate([own, along_z(own, 4)])
        near = jnp.concatenate([two, along_z(two, 2)])
        far = along_z(near, 1)
        return [near, other_core(near), far, other_core(far)]

    head_blocks = gathered(head)
    tail_blocks = gathered(tail)

    last, first = final_vectors[:, row_count - HALF :], final_vectors[:, :HALF]
    before = lax.ppermute(last, ("zh", "x"), [(i, i + 1) for i in range(7)])
    after = lax.ppermute(first, ("zh", "x"), [(i + 1, i) for i in range(7)])
    wide = jnp.concatenate([before, final_vectors, after], axis=1)
    windows = jnp.stack([wide[:, HALF * k : HALF * (k + 3)] for k in range(4)])
    panel = lax.all_to_all(windows, "y", 0, 0)

    def product(count, vecs, bands):
        depth = 16 * own_rows
        return pl.pallas_call(
            functools.partial(product_kernel, row_count, count),
            grid=(count,),
            out_shape=jax.ShapeDtypeStruct((16, count, 2, lines, vectors // 8), bf16),
            in_specs=[SMEM, VMEM] + [VMEM] * (len(vecs) + len(bands)),
            out_specs=pl.BlockSpec((16, 1, 2, lines, vectors // 8), lambda p: (0, p, 0, 0, 0)),
            scratch_shapes=[pltpu.VMEM((depth, 3 * HALF), bf16), pltpu.VMEM((depth, vectors), bf16)],
            compiler_params=pltpu.CompilerParams(vmem_limit_bytes=24 * 1024 * 1024),
            cost_estimate=pl.CostEstimate(
                flops=2 * count * 4 * lines * depth * (3 * HALF + vectors),
                bytes_accessed=4_000_000 * count,
                transcendentals=0,
            ),
            name=f"product_{count}",
        )(band_offsets, panel, *vecs, *bands)

    def summed(partial):
        parts = lax.all_to_all(partial, ("x", "y"), 0, 0)
        total = jnp.sum(parts.astype(jnp.float32), axis=0)
        mine = jnp.where(zh == 0, total[:, 0], total[:, 1])
        theirs = jnp.where(zh == 0, total[:, 1], total[:, 0]).astype(bf16)
        got = lax.ppermute(theirs, "zh", [(0, 1), (1, 0)])
        return (mine + got.astype(jnp.float32)).astype(bf16)

    first_sum = summed(product(1, head_blocks, []))
    rest_sum = summed(product(2, head_blocks, tail_blocks))
    return jnp.concatenate([first_sum, rest_sum])


def solution(mesh):
    fine = Mesh(mesh.devices.reshape(2, 4, 4, 8, 2), AXES)
    cfg, col = AXES[:2], AXES[2:]
    placed = (P(None, AXES, None), P(AXES, None), P(col, cfg), P(cfg))
    return jax.shard_map(
        shards, mesh=fine, in_specs=placed, out_specs=P(None, col, cfg), check_vma=False
    )
```
